32 devices in a mesh: req: 4 (over x, core), gx: 4 (over z), gy: 2 (over y).
Axes of the slice: x: 2, y: 2, z: 4, core: 2. Of those that a mesh axis runs over, the one named last changes fastest.
Arguments:
- hidden: bfloat16 [3072, 4096], P(('req', 'gx'), 'gy')
- ln_gain: float32 [4096], P('gy'), may hold values from 0.25 to 1.75
- w_qkv: bfloat16 [4096, 32, 384], P('gy', 'gx'), may hold values from -0.09375 to 0.09375
- w_out: bfloat16 [4096, 4096], P('gx', 'gy'), may hold values from -0.375 to 0.375
- kv_cache: bfloat16 [8, 2176, 2, 4096], P('req', 'gy', None, 'gx')
- cache_len: int32 [8], P('req'), may hold values from 0 to 1792, as said below
Outputs:
- mixed: bfloat16 [3072, 4096], P(('req', 'gx'), 'gy')
- cache_out: bfloat16 [8, 2176, 2, 4096], P('req', 'gy', None, 'gx')
The draws below stay inside these ranges and needn't reach their ends.
Inputs may be any that keep to these rules, and one draw needn't show every extreme that they name: `cache_len`: cached lengths are heavy-tailed; some request has exactly 1792.
All inputs are finite; a program needn't handle non-finite values.
Results may differ from the reference program's by a relative error of at most 0.04.
Values may be sent and summed in bfloat16 or wider, within the bound.
A program may use at most 128 MiB of HBM per device.

```python
import math
import jax
import jax.numpy as jnp
from jax import lax

D = 4096
H = 32
HD = 128
GROUP = 384
PAST = 1792
REQS = 8
TOKENS = 3072
CAP = 2176
N_GY = 2


def draw_hidden(key, part):
    first = jax.random.fold_in(key, 0)
    columns = jnp.arange(D, dtype=jnp.float32)
    column_scale = 1.0 + 2.0 * columns / D
    values = jax.random.normal(first, (TOKENS, D), jnp.float32) * column_scale[None, :]
    return values.astype(jnp.bfloat16)


def draw_kv_cache(key, part):
    first = jax.random.fold_in(key, 0)
    values = jax.random.normal(first, (REQS, CAP, 2, D), jnp.float32)
    return values.astype(jnp.bfloat16)


def draw_cache_len(key, part):
    first, second, third = jax.random.split(key, 3)
    divisor = jax.random.randint(first, (REQS,), 1, 17)
    lengths = jax.random.randint(second, (REQS,), 0, PAST + 1) // divisor
    chosen = jax.random.randint(third, (), 0, REQS)
    lengths = jnp.where(jnp.arange(REQS, dtype=jnp.int32) == chosen, PAST, lengths)
    return lengths.astype(jnp.int32)


def shard_levels(key, shape, cuts, low, high):
    loudness = 1.0
    for axis_at, blocks in cuts:
        heights = jax.random.uniform(jax.random.fold_in(jax.random.fold_in(key, 6), axis_at), (blocks,), jnp.float32, low / len(cuts), high / len(cuts))
        loudness = loudness * jnp.repeat(jnp.exp(heights), shape[axis_at] // blocks).reshape((-1,) + (1,) * (len(shape) - 1 - axis_at))
    return loudness


def noise(own_key, dims, scale, bound, pieces=(), kind=jnp.bfloat16):
    drawn = scale * jax.random.normal(own_key, dims, jnp.float32)
    if pieces:
        drawn = drawn * shard_levels(own_key, dims, pieces, -0.22, 0.18)
    return jnp.clip(drawn, -bound, bound).astype(kind)


def setup_inputs(seed: int = 0) -> dict:
    streams_of = jax.random.split(jax.random.key(seed), 7)
    return {
        "hidden": draw_hidden(jax.random.fold_in(streams_of[6], 71), 0),
        "ln_gain": jnp.clip(1.0 + 0.15 * jax.random.normal(streams_of[1], (D,), jnp.float32), 0.25, 1.75),
        "w_qkv": noise(streams_of[2], (D, H, 3 * HD), D ** -0.5, 0.09375, ((0, 2), (1, 4))),
        "w_out": noise(streams_of[3], (D, D), (D // 16) ** -0.5, 0.375, ((0, 4), (1, 2))),
        "kv_cache": draw_kv_cache(jax.random.fold_in(streams_of[6], 71), 0),
        "cache_len": draw_cache_len(jax.random.fold_in(streams_of[6], 71), 0),
    }


norm_eps = 1e-05
floor_score = -1e+30

def attend(query, keys, values, length, slopes):
    count = query.shape[0]
    places = keys.shape[0]
    scale = 1.0 / math.sqrt(query.shape[2])
    scores = jnp.einsum('chd,phd->chp', query.astype(jnp.float32), keys.astype(jnp.float32)) * scale
    distance = (length + jnp.arange(count, dtype=jnp.int32))[:, None] - jnp.arange(places, dtype=jnp.int32)[None, :]
    valid = distance >= 0
    scores = scores - slopes[None, :, None] * distance.astype(jnp.float32)[:, None, :]
    scores = jnp.where(valid[:, None, :], scores, floor_score)
    highest = lax.optimization_barrier(jnp.max(scores, axis=-1, keepdims=True))
    weights = jnp.where(valid[:, None, :], jnp.exp(scores - highest), 0.0)
    totals = lax.optimization_barrier(jnp.sum(weights, axis=-1))
    rounded = weights.astype(jnp.bfloat16)
    summed = jnp.einsum('chp,phd->chd', rounded.astype(jnp.float32), values.astype(jnp.float32))
    return summed / totals[..., None]

def reference(hidden, ln_gain, w_qkv, w_out, kv_cache, cache_len):
    hidden_f = hidden.astype(jnp.float32)
    mean = lax.optimization_barrier(jnp.mean(hidden_f, axis=1, keepdims=True))
    var = lax.optimization_barrier(jnp.mean(hidden_f * hidden_f, axis=1, keepdims=True)) - mean * mean
    normed = ((hidden_f - mean) * lax.rsqrt(var + norm_eps) * ln_gain[None, :]).astype(jnp.bfloat16)
    flat = w_qkv.reshape(D, 3 * D)
    span = D // N_GY
    summed = jnp.zeros((TOKENS, 3 * D), jnp.float32)
    for block in range(N_GY):
        part = jnp.dot(normed[:, block * span:(block + 1) * span], flat[block * span:(block + 1) * span], preferred_element_type=jnp.float32)
        part = lax.optimization_barrier(part.astype(jnp.bfloat16)).astype(jnp.float32)
        summed = summed + part
    qkv = summed.astype(jnp.bfloat16).reshape(REQS, GROUP, H, 3 * HD)
    slopes = jnp.exp2(-8.0 * (jnp.arange(H, dtype=jnp.int32) + 1).astype(jnp.float32) / H)

    def one_request(items):
        row_qkv, cache, length = items
        query = row_qkv[:, :, :HD]
        fresh = jnp.stack([row_qkv[:, :, HD:2 * HD].reshape(GROUP, D), row_qkv[:, :, 2 * HD:].reshape(GROUP, D)], axis=1)
        offset = jnp.arange(CAP, dtype=jnp.int32) - length
        inside = (offset >= 0) & (offset < GROUP)
        taken = jnp.take(fresh, jnp.clip(offset, 0, GROUP - 1), axis=0)
        updated = jnp.where(inside[:, None, None], taken, cache)
        keys = updated[:, 0].reshape(CAP, H, HD)
        values = updated[:, 1].reshape(CAP, H, HD)
        result = attend(query, keys, values, length, slopes).astype(jnp.bfloat16).reshape(GROUP, D)
        return (result, updated)
    attn, cache_out = lax.map(one_request, (qkv, kv_cache, cache_len))
    mixed = (jnp.dot(attn.reshape(TOKENS, D), w_out, preferred_element_type=jnp.float32) + hidden_f).astype(jnp.bfloat16)
    return (mixed, cache_out)
```

```python
import math

import jax
import jax.numpy as jnp
from jax import lax
from jax.sharding import PartitionSpec as P

D = 4096
CHUNKS = 1

norm_eps = 1e-05
floor_score = -1e30


def other(value):
    return lax.ppermute(value, "gy", [(0, 1), (1, 0)])


def sum_gy(value):
    if lax.axis_size("gy") == 2:
        total = value.astype(jnp.float32) + other(value).astype(jnp.float32)
        return total.astype(value.dtype)
    return lax.psum(value, "gy")


def scatter_gy(value):
    n = lax.axis_size("gy")
    if n == 2:
        half = value.shape[1] // 2
        me = lax.axis_index("gy")
        low, high = value[:, :half], value[:, half:]
        first = me == 0
        arrived = other(jnp.where(first, high, low)).astype(jnp.float32)
        own = jnp.where(first, low, high).astype(jnp.float32)
        return (own + arrived).astype(value.dtype)
    return lax.psum_scatter(value, "gy", scatter_dimension=1, tiled=True)


def combine(top, total, accum):
    if lax.axis_size("gy") == 2:
        safe = jnp.where(total > 0, total, 1.0)
        part = (accum / safe[..., None]).astype(jnp.bfloat16)
        stats = jnp.stack([top, total])
        far_stats = other(stats)
        far_part = other(part)
        overall = jnp.maximum(top, far_stats[0])
        mine = jnp.exp(top - overall) * total
        far = jnp.exp(far_stats[0] - overall) * far_stats[1]
        joined = mine + far
        return (
            part.astype(jnp.float32) * (mine / joined)[..., None]
            + far_part.astype(jnp.float32) * (far / joined)[..., None]
        ).astype(jnp.bfloat16)
    factor = jnp.exp(top - lax.pmax(top, "gy"))
    totals = lax.psum(total * factor, "gy")
    accums = lax.psum((accum * factor[..., None]).astype(jnp.bfloat16), "gy")
    return (accums.astype(jnp.float32) / totals[..., None]).astype(jnp.bfloat16)


def split_cache(cache):
    requests, block, _, width = cache.shape
    size = math.gcd(2 * block, 128)
    rows = cache.reshape(requests, 2 * block // size, size, width)
    target = jnp.arange(size)[:, None]
    source = jnp.arange(size)[None, :]
    half = size // 2
    pick = (source == 2 * (target % half) + target // half).astype(cache.dtype)
    ordered = jnp.einsum("ks,rbsd->rbkd", pick, rows, preferred_element_type=jnp.float32)
    ordered = ordered.astype(cache.dtype)
    return (
        ordered[:, :, :half].reshape(requests, block, width),
        ordered[:, :, half:].reshape(requests, block, width),
    )


def partial_attend(query, keys, values, valid, distance, slopes, scale):
    scores = jnp.einsum("chd,phd->chp", query, keys, preferred_element_type=jnp.float32) * scale
    scores = scores - slopes[None, :, None] * distance.astype(jnp.float32)[:, None, :]
    scores = jnp.where(valid[:, None, :], scores, floor_score)
    highest = jnp.max(scores, axis=-1)
    weights = jnp.where(valid[:, None, :], jnp.exp(scores - highest[..., None]), 0.0)
    totals = jnp.sum(weights, axis=-1)
    accum = jnp.einsum(
        "chp,phd->chd", weights.astype(jnp.bfloat16), values, preferred_element_type=jnp.float32
    )
    return (highest, totals, accum)


def shards(hidden, ln_gain, w_qkv, w_out, kv_cache, cache_len):
    local_rows = hidden.shape[0]
    gx_n = lax.axis_size("gx")
    gy_n = lax.axis_size("gy")
    gy = lax.axis_index("gy")
    hidden_f = hidden.astype(jnp.float32)
    piece = local_rows // CHUNKS
    gathered = [
        lax.all_gather(hidden[c * piece : (c + 1) * piece], "gx", axis=0) for c in range(CHUNKS)
    ]
    sums = sum_gy(jnp.stack([jnp.sum(hidden_f, axis=1), jnp.sum(hidden_f * hidden_f, axis=1)]))
    mean = sums[0] / D
    rstd = lax.rsqrt(sums[1] / D - mean * mean + norm_eps)
    stats = lax.all_gather(jnp.stack([mean, rstd]), "gx", axis=0)

    depth, local_heads = w_qkv.shape[:2]
    head_size = w_qkv.shape[2] // 3
    width = local_heads * head_size
    w_q = w_qkv[:, :, :head_size].reshape(depth, width)
    w_k = w_qkv[:, :, head_size : 2 * head_size].reshape(depth, width)
    w_v = w_qkv[:, :, 2 * head_size :].reshape(depth, width)

    requests = cache_len.shape[0]
    share = gx_n // requests
    group = share * local_rows
    rows = share * piece
    part = rows // gy_n
    block = kv_cache.shape[1]
    old_keys, old_values = split_cache(kv_cache)

    queries, keys, values = [], [], []
    for c in range(CHUNKS):
        st = stats[:, :, c * piece : (c + 1) * piece]
        normed = (
            (gathered[c].astype(jnp.float32) - st[:, 0, :, None]) * st[:, 1, :, None] * ln_gain
        ).astype(jnp.bfloat16)
        normed = normed.reshape(gx_n * piece, depth)
        kv = [
            jnp.dot(normed, w, preferred_element_type=jnp.float32)
            .astype(jnp.bfloat16)
            .reshape(requests, rows, width)
            for w in (w_k, w_v)
        ]
        q = jnp.dot(normed, w_q, preferred_element_type=jnp.float32).astype(jnp.bfloat16)
        keys.append(scatter_gy(kv[0]))
        queries.append(sum_gy(q).reshape(requests, rows, local_heads, head_size))
        values.append(scatter_gy(kv[1]))

    flat = jnp.arange(rows, dtype=jnp.int32)
    tokens = [(flat // piece) * local_rows + c * piece + flat % piece for c in range(CHUNKS)]
    own = [lax.dynamic_slice_in_dim(t, gy * part, part) for t in tokens]
    own_tokens = jnp.concatenate(own)
    own_keys = jnp.concatenate(keys, axis=1)
    own_values = jnp.concatenate(values, axis=1)

    def whole(parts):
        full = lax.all_gather(parts, "gy", axis=0)
        full = full.reshape(gy_n, requests, CHUNKS, part, width).transpose(1, 2, 0, 3, 4)
        full = full.reshape(requests, CHUNKS, share, piece, width).transpose(0, 2, 1, 3, 4)
        return full.reshape(requests, group, width)

    fresh = jnp.stack([whole(own_keys), whole(own_values)], axis=2)
    window = min(group, block)
    padded = jnp.pad(fresh, ((0, 0), (window, window), (0, 0), (0, 0)))
    updated = kv_cache
    for r in range(requests):
        away = cache_len[r] - gy * block
        begin = jnp.clip(away, 0, block - window)
        taken = lax.dynamic_slice_in_dim(
            padded[r], jnp.clip(window + begin - away, 0, group + window), window
        )
        offset = begin - away + jnp.arange(window, dtype=jnp.int32)
        inside = (offset >= 0) & (offset < group)
        old = lax.dynamic_slice_in_dim(kv_cache[r], begin, window)
        new = jnp.where(inside[:, None, None], taken, old)
        updated = lax.dynamic_update_slice(updated, new[None], (r, begin, 0, 0))

    head_ids = lax.axis_index("gx") * local_heads + jnp.arange(local_heads, dtype=jnp.int32)
    slopes = jnp.exp2(-8.0 * (head_ids + 1).astype(jnp.float32) / (local_heads * gx_n))
    scale = 1.0 / math.sqrt(head_size)
    positions = gy * block + jnp.arange(block, dtype=jnp.int32)
    results = []
    full_keys = jnp.concatenate([old_keys, own_keys], axis=1)
    full_values = jnp.concatenate([old_values, own_values], axis=1)
    full_keys = full_keys.reshape(requests, -1, local_heads, head_size)
    full_values = full_values.reshape(requests, -1, local_heads, head_size)
    for c in range(CHUNKS):
        parts = []
        for r in range(requests):
            length = cache_len[r]
            places = jnp.concatenate([positions, length + own_tokens])
            distance = (length + tokens[c])[:, None] - places[None, :]
            cached = jnp.concatenate([positions < length, own_tokens >= 0])
            valid = (distance >= 0) & cached[None, :]
            parts.append(
                partial_attend(
                    queries[c][r], full_keys[r], full_values[r], valid, distance, slopes, scale
                )
            )
        top, total, accum = (jnp.stack(p) for p in zip(*parts))
        attn = combine(top, total, accum).reshape(requests * rows, width)
        projected = lax.psum_scatter(
            jnp.dot(attn, w_out, preferred_element_type=jnp.float32).astype(jnp.bfloat16),
            "gx",
            scatter_dimension=0,
            tiled=True,
        ).astype(jnp.float32)
        results.append(projected)
    mixed = (jnp.concatenate(results) + hidden_f).astype(jnp.bfloat16)
    return (mixed, updated)


def solution(mesh):
    in_specs = (
        P(("req", "gx"), "gy"),
        P("gy"),
        P("gy", "gx", None),
        P("gx", "gy"),
        P("req", "gy", None, "gx"),
        P("req"),
    )
    out_specs = (P(("req", "gx"), "gy"), P("req", "gy", None, "gx"))
    return jax.shard_map(shards, mesh=mesh, in_specs=in_specs, out_specs=out_specs, check_vma=False)
```

```python
import functools
import math

import jax
import jax.numpy as jnp
from jax import lax
from jax.experimental import pallas as pl
from jax.experimental.pallas import tpu as pltpu
from jax.sharding import PartitionSpec as P

D = 4096
CHUNKS = 2

norm_eps = 1e-05
floor_score = -1e30


def other(value):
    return lax.ppermute(value, "gy", [(0, 1), (1, 0)])


def sum_gy(value):
    if lax.axis_size("gy") == 2:
        total = value.astype(jnp.float32) + other(value).astype(jnp.float32)
        return total.astype(value.dtype)
    return lax.psum(value, "gy")


def scatter_gy(value):
    n = lax.axis_size("gy")
    if n == 2:
        half = value.shape[1] // 2
        me = lax.axis_index("gy")
        low, high = value[:, :half], value[:, half:]
        first = me == 0
        arrived = other(jnp.where(first, high, low)).astype(jnp.float32)
        own = jnp.where(first, low, high).astype(jnp.float32)
        return (own + arrived).astype(value.dtype)
    return lax.psum_scatter(value, "gy", scatter_dimension=1, tiled=True)


def combine(part, level):
    requests, rows, heads = level.shape
    part = part.reshape(requests, rows, heads, -1)
    if lax.axis_size("gy") == 2:
        far_level = other(level)
        far_part = other(part.reshape(requests, rows, -1)).reshape(part.shape)
        overall = jnp.maximum(level, far_level)
        mine, far = jnp.exp(level - overall), jnp.exp(far_level - overall)
        joined = mine + far
        return (
            part.astype(jnp.float32) * (mine / joined)[..., None]
            + far_part.astype(jnp.float32) * (far / joined)[..., None]
        ).astype(jnp.bfloat16)
    factor = jnp.exp(level - lax.pmax(level, "gy"))
    totals = lax.psum(factor, "gy")
    accums = lax.psum((part.astype(jnp.float32) * factor[..., None]).astype(jnp.bfloat16), "gy")
    return (accums.astype(jnp.float32) / totals[..., None]).astype(jnp.bfloat16)


def split_cache(cache):
    requests, block, _, width = cache.shape
    size = math.gcd(2 * block, 128)
    rows = cache.reshape(requests, 2 * block // size, size, width)
    target = jnp.arange(size)[:, None]
    source = jnp.arange(size)[None, :]
    half = size // 2
    pick = (source == 2 * (target % half) + target // half).astype(cache.dtype)
    ordered = jnp.einsum("ks,rbsd->rbkd", pick, rows, preferred_element_type=jnp.float32)
    ordered = ordered.astype(cache.dtype)
    return (
        ordered[:, :, :half].reshape(requests, block, width),
        ordered[:, :, half:].reshape(requests, block, width),
    )


def attend_kernel(
    scale, info, slopes, q_ref, ok_ref, ov_ref, nk_ref, nv_ref, c_ref, t_ref, part_ref, level_ref
):
    r, h = pl.program_id(0), pl.program_id(1)
    slope = slopes[h]
    away = info[0] - info[1 + r]
    block = ok_ref.shape[1]
    offset = lax.broadcasted_iota(jnp.int32, (1, block), 1) + away
    bias = jnp.where(offset < 0, slope * offset.astype(jnp.float32), floor_score)
    dims = (((1,), (1,)), ((), ()))
    q = q_ref[0]
    old = lax.dot_general(q, ok_ref[0], dims, preferred_element_type=jnp.float32) * scale + bias
    token = t_ref[...]
    new = lax.dot_general(q, nk_ref[0], dims, preferred_element_type=jnp.float32) * scale
    new = jnp.where(token <= c_ref[...], new + slope * token.astype(jnp.float32), floor_score)
    top = jnp.maximum(jnp.max(old, axis=1, keepdims=True), jnp.max(new, axis=1, keepdims=True))
    top = jnp.maximum(top, 0.1 * floor_score)
    old = jnp.exp(old - top)
    new = jnp.exp(new - top)
    total = jnp.sum(old, axis=1, keepdims=True) + jnp.sum(new, axis=1, keepdims=True)
    accum = jnp.dot(old.astype(jnp.bfloat16), ov_ref[0], preferred_element_type=jnp.float32)
    accum += jnp.dot(new.astype(jnp.bfloat16), nv_ref[0], preferred_element_type=jnp.float32)
    some = total > 0
    safe = jnp.where(some, total, 1.0)
    part_ref[0] = (accum / safe).astype(part_ref.dtype)
    level = jnp.where(some, top + jnp.log(safe), floor_score)
    lane = lax.broadcasted_iota(jnp.int32, level_ref.shape[1:], 1)

    @pl.when(h == 0)
    def _():
        level_ref[...] = jnp.zeros_like(level_ref)

    level_ref[0] = jnp.where(lane == h, level, level_ref[0])


def attend(info, slopes, q, old_k, old_v, new_k, new_v, tokens, own_tokens, heads):
    requests, rows, width = q.shape
    size = width // heads
    head = lambda n: pl.BlockSpec((1, n, size), lambda r, h, *_: (r, 0, h))
    fixed = lambda shape: pl.BlockSpec(shape, lambda r, h, *_: (0, 0))
    block, own = old_k.shape[1], new_k.shape[1]
    lanes = 128
    part, level = pl.pallas_call(
        functools.partial(attend_kernel, 1.0 / math.sqrt(size)),
        grid_spec=pltpu.PrefetchScalarGridSpec(
            num_scalar_prefetch=2,
            grid=(requests, heads),
            in_specs=[
                head(rows),
                head(block),
                head(block),
                head(own),
                head(own),
                fixed((rows, 1)),
                fixed((1, own)),
            ],
            out_specs=[head(rows), pl.BlockSpec((1, rows, lanes), lambda r, h, *_: (r, 0, 0))],
        ),
        out_shape=[
            jax.ShapeDtypeStruct((requests, rows, width), jnp.bfloat16),
            jax.ShapeDtypeStruct((requests, rows, lanes), jnp.float32),
        ],
        compiler_params=pltpu.CompilerParams(vmem_limit_bytes=32 * 1024 * 1024),
        cost_estimate=pl.CostEstimate(
            flops=4 * requests * rows * (block + own) * width,
            bytes_accessed=4 * requests * (block + own + rows) * width,
            transcendentals=requests * rows * (block + own) * heads,
        ),
    )(info, slopes, q, old_k, old_v, new_k, new_v, tokens[:, None], own_tokens[None, :])
    return part, level[:, :, :heads]


def shards(hidden, ln_gain, w_qkv, w_out, kv_cache, cache_len):
    local_rows = hidden.shape[0]
    gx_n = lax.axis_size("gx")
    gy_n = lax.axis_size("gy")
    gy = lax.axis_index("gy")
    hidden_f = hidden.astype(jnp.float32)
    piece = local_rows // CHUNKS
    gathered = [
        lax.all_gather(hidden[c * piece : (c + 1) * piece], "gx", axis=0) for c in range(CHUNKS)
    ]
    sums = sum_gy(jnp.stack([jnp.sum(hidden_f, axis=1), jnp.sum(hidden_f * hidden_f, axis=1)]))
    mean = sums[0] / D
    rstd = lax.rsqrt(sums[1] / D - mean * mean + norm_eps)
    stats = lax.all_gather(jnp.stack([mean, rstd]), "gx", axis=0)

    depth, local_heads = w_qkv.shape[:2]
    head_size = w_qkv.shape[2] // 3
    width = local_heads * head_size
    w_q = w_qkv[:, :, :head_size].reshape(depth, width)
    w_k = w_qkv[:, :, head_size : 2 * head_size].reshape(depth, width)
    w_v = w_qkv[:, :, 2 * head_size :].reshape(depth, width)

    requests = cache_len.shape[0]
    share = gx_n // requests
    group = share * local_rows
    rows = share * piece
    own_rows = rows // gy_n
    block = kv_cache.shape[1]
    queries, keys, values = [], [], []
    for c in range(CHUNKS):
        st = stats[:, :, c * piece : (c + 1) * piece]
        normed = (
            (gathered[c].astype(jnp.float32) - st[:, 0, :, None]) * st[:, 1, :, None] * ln_gain
        ).astype(jnp.bfloat16)
        normed = normed.reshape(gx_n * piece, depth)
        kv = [
            jnp.dot(normed, w, preferred_element_type=jnp.float32)
            .astype(jnp.bfloat16)
            .reshape(requests, rows, width)
            for w in (w_k, w_v)
        ]
        q = jnp.dot(normed, w_q, preferred_element_type=jnp.float32).astype(jnp.bfloat16)
        if c == 0:
            q, kv_cache = lax.optimization_barrier((q, kv_cache))
        keys.append(scatter_gy(kv[0]))
        values.append(scatter_gy(kv[1]))
        queries.append(sum_gy(q).reshape(requests, rows, width))
    old_keys, old_values = split_cache(kv_cache)

    flat = jnp.arange(rows, dtype=jnp.int32)
    tokens = [(flat // piece) * local_rows + c * piece + flat % piece for c in range(CHUNKS)]
    own = [lax.dynamic_slice_in_dim(t, gy * own_rows, own_rows) for t in tokens]
    own_tokens = jnp.concatenate(own)
    own_keys = jnp.concatenate(keys, axis=1)
    own_values = jnp.concatenate(values, axis=1)

    def whole(parts):
        full = lax.all_gather(parts, "gy", axis=0)
        full = full.reshape(gy_n, requests, CHUNKS, own_rows, width).transpose(1, 2, 0, 3, 4)
        full = full.reshape(requests, CHUNKS, share, piece, width).transpose(0, 2, 1, 3, 4)
        return full.reshape(requests, group, width)

    sent_keys, sent_values, queries[-1] = lax.optimization_barrier(
        (own_keys, own_values, queries[-1])
    )
    fresh = jnp.stack([whole(sent_keys), whole(sent_values)], axis=2)
    window = min(group, block)
    padded = jnp.pad(fresh, ((0, 0), (window, window), (0, 0), (0, 0)))
    updated = kv_cache
    for r in range(requests):
        away = cache_len[r] - gy * block
        begin = jnp.clip(away, 0, block - window)
        taken = lax.dynamic_slice_in_dim(
            padded[r], jnp.clip(window + begin - away, 0, group + window), window
        )
        offset = begin - away + jnp.arange(window, dtype=jnp.int32)
        inside = (offset >= 0) & (offset < group)
        old = lax.dynamic_slice_in_dim(kv_cache[r], begin, window)
        new = jnp.where(inside[:, None, None], taken, old)
        updated = lax.dynamic_update_slice(updated, new[None], (r, begin, 0, 0))

    head_ids = lax.axis_index("gx") * local_heads + jnp.arange(local_heads, dtype=jnp.int32)
    slopes = jnp.exp2(-8.0 * (head_ids + 1).astype(jnp.float32) / (local_heads * gx_n))
    info = jnp.concatenate([(gy * block)[None].astype(jnp.int32), cache_len])
    results = []
    for c in range(CHUNKS):
        part, level = attend(
            info,
            slopes,
            queries[c],
            old_keys,
            old_values,
            own_keys,
            own_values,
            tokens[c],
            own_tokens,
            local_heads,
        )
        attn = combine(part, level).reshape(requests * rows, width)
        projected = lax.psum_scatter(
            jnp.dot(attn, w_out, preferred_element_type=jnp.float32).astype(jnp.bfloat16),
            "gx",
            scatter_dimension=0,
            tiled=True,
        ).astype(jnp.float32)
        results.append(projected)
    mixed = (jnp.concatenate(results) + hidden_f).astype(jnp.bfloat16)
    return (mixed, updated)


def solution(mesh):
    in_specs = (
        P(("req", "gx"), "gy"),
        P("gy"),
        P("gy", "gx", None),
        P("gx", "gy"),
        P("req", "gy", None, "gx"),
        P("req"),
    )
    out_specs = (P(("req", "gx"), "gy"), P("req", "gy", None, "gx"))
    return jax.shard_map(shards, mesh=mesh, in_specs=in_specs, out_specs=out_specs, check_vma=False)
```

```python
import functools
import math

import jax
import jax.numpy as jnp
from jax import lax
from jax.experimental import pallas as pl
from jax.experimental.pallas import tpu as pltpu
from jax.sharding import PartitionSpec as P

D = 4096
CHUNKS = 2

norm_eps = 1e-05
floor_score = -1e30


def other(value):
    return lax.ppermute(value, "gy", [(0, 1), (1, 0)])


def sum_gy(value):
    if lax.axis_size("gy") == 2:
        total = value.astype(jnp.float32) + other(value).astype(jnp.float32)
        return total.astype(value.dtype)
    return lax.psum(value, "gy")


def scatter_gy(value):
    n = lax.axis_size("gy")
    if n == 2:
        half = value.shape[1] // 2
        me = lax.axis_index("gy")
        low, high = value[:, :half], value[:, half:]
        first = me == 0
        arrived = other(jnp.where(first, high, low)).astype(jnp.float32)
        own = jnp.where(first, low, high).astype(jnp.float32)
        return (own + arrived).astype(value.dtype)
    return lax.psum_scatter(value, "gy", scatter_dimension=1, tiled=True)


def combine(part, level):
    requests, rows, heads = level.shape
    part = part.reshape(requests, rows, heads, -1)
    if lax.axis_size("gy") == 2:
        far_level = other(level)
        far_part = other(part.reshape(requests, rows, -1)).reshape(part.shape)
        overall = jnp.maximum(level, far_level)
        mine, far = jnp.exp(level - overall), jnp.exp(far_level - overall)
        joined = mine + far
        return (
            part.astype(jnp.float32) * (mine / joined)[..., None]
            + far_part.astype(jnp.float32) * (far / joined)[..., None]
        ).astype(jnp.bfloat16)
    factor = jnp.exp(level - lax.pmax(level, "gy"))
    totals = lax.psum(factor, "gy")
    accums = lax.psum((part.astype(jnp.float32) * factor[..., None]).astype(jnp.bfloat16), "gy")
    return (accums.astype(jnp.float32) / totals[..., None]).astype(jnp.bfloat16)


def copy_kernel(source, after, target, sem):
    copy = pltpu.make_async_copy(source, target, sem)
    copy.start()
    copy.wait()


def copy_after(source, after):
    return pl.pallas_call(
        copy_kernel,
        out_shape=jax.ShapeDtypeStruct(source.shape, source.dtype),
        in_specs=[pl.BlockSpec(memory_space=pl.ANY)] * 2,
        out_specs=pl.BlockSpec(memory_space=pl.ANY),
        scratch_shapes=[pltpu.SemaphoreType.DMA],
        cost_estimate=pl.CostEstimate(
            flops=0, bytes_accessed=4 * source.size, transcendentals=0
        ),
    )(source, after)


def split_cache(cache):
    requests, block, _, width = cache.shape
    size = math.gcd(2 * block, 128)
    rows = cache.reshape(requests, 2 * block // size, size, width)
    target = jnp.arange(size)[:, None]
    source = jnp.arange(size)[None, :]
    half = size // 2
    pick = (source == 2 * (target % half) + target // half).astype(cache.dtype)
    ordered = jnp.einsum("ks,rbsd->rbkd", pick, rows, preferred_element_type=jnp.float32)
    ordered = ordered.astype(cache.dtype)
    return (
        ordered[:, :, :half].reshape(requests, block, width),
        ordered[:, :, half:].reshape(requests, block, width),
    )


def attend_kernel(
    scale, info, slopes, q_ref, ok_ref, ov_ref, nk_ref, nv_ref, c_ref, t_ref, part_ref, level_ref
):
    r, h = pl.program_id(0), pl.program_id(1)
    slope = slopes[h]
    away = info[0] - info[1 + r]
    block = ok_ref.shape[1]
    offset = lax.broadcasted_iota(jnp.int32, (1, block), 1) + away
    bias = jnp.where(offset < 0, slope * offset.astype(jnp.float32), floor_score)
    dims = (((1,), (1,)), ((), ()))
    q = q_ref[0]
    old = lax.dot_general(q, ok_ref[0], dims, preferred_element_type=jnp.float32) * scale + bias
    token = t_ref[...]
    new = lax.dot_general(q, nk_ref[0], dims, preferred_element_type=jnp.float32) * scale
    new = jnp.where(token <= c_ref[...], new + slope * token.astype(jnp.float32), floor_score)
    top = jnp.maximum(jnp.max(old, axis=1, keepdims=True), jnp.max(new, axis=1, keepdims=True))
    top = jnp.maximum(top, 0.1 * floor_score)
    old = jnp.exp(old - top)
    new = jnp.exp(new - top)
    total = jnp.sum(old, axis=1, keepdims=True) + jnp.sum(new, axis=1, keepdims=True)
    accum = jnp.dot(old.astype(jnp.bfloat16), ov_ref[0], preferred_element_type=jnp.float32)
    accum += jnp.dot(new.astype(jnp.bfloat16), nv_ref[0], preferred_element_type=jnp.float32)
    some = total > 0
    safe = jnp.where(some, total, 1.0)
    part_ref[0] = (accum / safe).astype(part_ref.dtype)
    level = jnp.where(some, top + jnp.log(safe), floor_score)
    lane = lax.broadcasted_iota(jnp.int32, level_ref.shape[1:], 1)

    @pl.when(h == 0)
    def _():
        level_ref[...] = jnp.zeros_like(level_ref)

    level_ref[0] = jnp.where(lane == h, level, level_ref[0])


def attend(info, slopes, q, old_k, old_v, new_k, new_v, tokens, own_tokens, heads):
    requests, rows, width = q.shape
    size = width // heads
    head = lambda n: pl.BlockSpec((1, n, size), lambda r, h, *_: (r, 0, h))
    fixed = lambda shape: pl.BlockSpec(shape, lambda r, h, *_: (0, 0))
    block, own = old_k.shape[1], new_k.shape[1]
    lanes = 128
    part, level = pl.pallas_call(
        functools.partial(attend_kernel, 1.0 / math.sqrt(size)),
        grid_spec=pltpu.PrefetchScalarGridSpec(
            num_scalar_prefetch=2,
            grid=(requests, heads),
            in_specs=[
                head(rows),
                head(block),
                head(block),
                head(own),
                head(own),
                fixed((rows, 1)),
                fixed((1, own)),
            ],
            out_specs=[head(rows), pl.BlockSpec((1, rows, lanes), lambda r, h, *_: (r, 0, 0))],
        ),
        out_shape=[
            jax.ShapeDtypeStruct((requests, rows, width), jnp.bfloat16),
            jax.ShapeDtypeStruct((requests, rows, lanes), jnp.float32),
        ],
        compiler_params=pltpu.CompilerParams(vmem_limit_bytes=32 * 1024 * 1024),
        cost_estimate=pl.CostEstimate(
            flops=4 * requests * rows * (block + own) * width,
            bytes_accessed=4 * requests * (block + own + rows) * width,
            transcendentals=requests * rows * (block + own) * heads,
        ),
    )(info, slopes, q, old_k, old_v, new_k, new_v, tokens[:, None], own_tokens[None, :])
    return part, level[:, :, :heads]


def shards(hidden, ln_gain, w_qkv, w_out, kv_cache, cache_len):
    local_rows = hidden.shape[0]
    gx_n = lax.axis_size("gx")
    gy_n = lax.axis_size("gy")
    gy = lax.axis_index("gy")
    hidden_f = hidden.astype(jnp.float32)
    piece = local_rows // CHUNKS
    gathered = [
        lax.all_gather(hidden[c * piece : (c + 1) * piece], "gx", axis=0) for c in range(CHUNKS)
    ]
    sums = sum_gy(jnp.stack([jnp.sum(hidden_f, axis=1), jnp.sum(hidden_f * hidden_f, axis=1)]))
    mean = sums[0] / D
    rstd = lax.rsqrt(sums[1] / D - mean * mean + norm_eps)
    stats = lax.all_gather(jnp.stack([mean, rstd]), "gx", axis=0)
    stats, split_from = lax.optimization_barrier((stats, kv_cache))
    old_keys, old_values = split_cache(split_from)

    depth, local_heads = w_qkv.shape[:2]
    head_size = w_qkv.shape[2] // 3
    width = local_heads * head_size
    w_q = w_qkv[:, :, :head_size].reshape(depth, width)
    w_k = w_qkv[:, :, head_size : 2 * head_size].reshape(depth, width)
    w_v = w_qkv[:, :, 2 * head_size :].reshape(depth, width)

    requests = cache_len.shape[0]
    share = gx_n // requests
    group = share * local_rows
    rows = share * piece
    own_rows = rows // gy_n
    block = kv_cache.shape[1]
    queries, keys, values = [], [], []
    for c in range(CHUNKS):
        st = stats[:, :, c * piece : (c + 1) * piece]
        normed = (
            (gathered[c].astype(jnp.float32) - st[:, 0, :, None]) * st[:, 1, :, None] * ln_gain
        ).astype(jnp.bfloat16)
        normed = normed.reshape(gx_n * piece, depth)
        kv = [
            jnp.dot(normed, w, preferred_element_type=jnp.float32)
            .astype(jnp.bfloat16)
            .reshape(requests, rows, width)
            for w in (w_k, w_v)
        ]
        q = jnp.dot(normed, w_q, preferred_element_type=jnp.float32).astype(jnp.bfloat16)
        last = q
        keys.append(scatter_gy(kv[0]))
        values.append(scatter_gy(kv[1]))
        queries.append(sum_gy(q).reshape(requests, rows, width))
        if c + 1 < CHUNKS:
            keys, values, queries, old_keys, old_values, gathered[c + 1] = (
                lax.optimization_barrier(
                    (keys, values, queries, old_keys, old_values, gathered[c + 1])
                )
            )

    flat = jnp.arange(rows, dtype=jnp.int32)
    tokens = [(flat // piece) * local_rows + c * piece + flat % piece for c in range(CHUNKS)]
    own = [lax.dynamic_slice_in_dim(t, gy * own_rows, own_rows) for t in tokens]
    own_tokens = jnp.concatenate(own)
    own_keys = jnp.concatenate(keys, axis=1)
    own_values = jnp.concatenate(values, axis=1)

    def whole(parts):
        full = lax.all_gather(parts, "gy", axis=0)
        full = full.reshape(gy_n, requests, CHUNKS, own_rows, width).transpose(1, 2, 0, 3, 4)
        full = full.reshape(requests, CHUNKS, share, piece, width).transpose(0, 2, 1, 3, 4)
        return full.reshape(requests, group, width)

    sent_keys, sent_values, queries = lax.optimization_barrier((own_keys, own_values, queries))
    fresh = jnp.stack([whole(sent_keys), whole(sent_values)], axis=2)
    window = min(group, block)
    padded = jnp.pad(fresh, ((0, 0), (window, window), (0, 0), (0, 0)))
    updated = copy_after(kv_cache, last)
    for r in range(requests):
        away = cache_len[r] - gy * block
        begin = jnp.clip(away, 0, block - window)
        start = jnp.clip(window + begin - away, 0, group + window)
        taken = lax.dynamic_slice(padded, (r, start, 0, 0), (1, window, 2, width))
        offset = begin - away + jnp.arange(window, dtype=jnp.int32)
        inside = (offset >= 0) & (offset < group)
        old = lax.dynamic_slice(kv_cache, (r, begin, 0, 0), (1, window, 2, width))
        new = jnp.where(inside[None, :, None, None], taken, old)
        updated = lax.dynamic_update_slice(updated, new, (r, begin, 0, 0))

    head_ids = lax.axis_index("gx") * local_heads + jnp.arange(local_heads, dtype=jnp.int32)
    slopes = jnp.exp2(-8.0 * (head_ids + 1).astype(jnp.float32) / (local_heads * gx_n))
    info = jnp.concatenate([(gy * block)[None].astype(jnp.int32), cache_len])
    results = []
    for c in range(CHUNKS):
        part, level = attend(
            info,
            slopes,
            queries[c],
            old_keys,
            old_values,
            own_keys,
            own_values,
            tokens[c],
            own_tokens,
            local_heads,
        )
        attn = combine(part, level).reshape(requests * rows, width)
        projected = lax.psum_scatter(
            jnp.dot(attn, w_out, preferred_element_type=jnp.float32).astype(jnp.bfloat16),
            "gx",
            scatter_dimension=0,
            tiled=True,
        ).astype(jnp.float32)
        results.append(projected)
    mixed = (jnp.concatenate(results) + hidden_f).astype(jnp.bfloat16)
    return (mixed, updated)


def solution(mesh):
    in_specs = (
        P(("req", "gx"), "gy"),
        P("gy"),
        P("gy", "gx", None),
        P("gx", "gy"),
        P("req", "gy", None, "gx"),
        P("req"),
    )
    out_specs = (P(("req", "gx"), "gy"), P("req", "gy", None, "gx"))
    return jax.shard_map(shards, mesh=mesh, in_specs=in_specs, out_specs=out_specs, check_vma=False)
```

```python
import functools
import math

import jax
import jax.numpy as jnp
from jax import lax
from jax.experimental import pallas as pl
from jax.experimental.pallas import tpu as pltpu
from jax.sharding import PartitionSpec as P

D = 4096
CHUNKS = 2

norm_eps = 1e-05
floor_score = -1e30


def other(value):
    return lax.ppermute(value, "gy", [(0, 1), (1, 0)])


def sum_gy(value):
    if lax.axis_size("gy") == 2:
        total = value.astype(jnp.float32) + other(value).astype(jnp.float32)
        return total.astype(value.dtype)
    return lax.psum(value, "gy")


def scatter_gy(value):
    n = lax.axis_size("gy")
    if n == 2:
        half = value.shape[1] // 2
        me = lax.axis_index("gy")
        low, high = value[:, :half], value[:, half:]
        first = me == 0
        arrived = other(jnp.where(first, high, low)).astype(jnp.float32)
        own = jnp.where(first, low, high).astype(jnp.float32)
        return (own + arrived).astype(value.dtype)
    return lax.psum_scatter(value, "gy", scatter_dimension=1, tiled=True)


def combine(part, level):
    requests, rows, heads = level.shape
    part = part.reshape(requests, rows, heads, -1)
    if lax.axis_size("gy") == 2:
        far_level = other(level)
        far_part = other(part.reshape(requests, rows, -1)).reshape(part.shape)
        overall = jnp.maximum(level, far_level)
        mine, far = jnp.exp(level - overall), jnp.exp(far_level - overall)
        joined = mine + far
        return (
            part.astype(jnp.float32) * (mine / joined)[..., None]
            + far_part.astype(jnp.float32) * (far / joined)[..., None]
        ).astype(jnp.bfloat16)
    factor = jnp.exp(level - lax.pmax(level, "gy"))
    totals = lax.psum(factor, "gy")
    accums = lax.psum((part.astype(jnp.float32) * factor[..., None]).astype(jnp.bfloat16), "gy")
    return (accums.astype(jnp.float32) / totals[..., None]).astype(jnp.bfloat16)


def split_cache(cache):
    requests, block, _, width = cache.shape
    size = math.gcd(2 * block, 128)
    rows = cache.reshape(requests, 2 * block // size, size, width)
    target = jnp.arange(size)[:, None]
    source = jnp.arange(size)[None, :]
    half = size // 2
    pick = (source == 2 * (target % half) + target // half).astype(cache.dtype)
    ordered = jnp.einsum("ks,rbsd->rbkd", pick, rows, preferred_element_type=jnp.float32)
    ordered = ordered.astype(cache.dtype)
    return (
        ordered[:, :, :half].reshape(requests, block, width),
        ordered[:, :, half:].reshape(requests, block, width),
    )


def attend_kernel(
    scale, info, slopes, q_ref, ok_ref, ov_ref, nk_ref, nv_ref, c_ref, t_ref, part_ref, level_ref
):
    r, h = pl.program_id(0), pl.program_id(1)
    slope = slopes[h]
    away = info[0] - info[1 + r]
    block = ok_ref.shape[1]
    offset = lax.broadcasted_iota(jnp.int32, (1, block), 1) + away
    bias = jnp.where(offset < 0, slope * offset.astype(jnp.float32), floor_score)
    dims = (((1,), (1,)), ((), ()))
    q = q_ref[0]
    old = lax.dot_general(q, ok_ref[0], dims, preferred_element_type=jnp.float32) * scale + bias
    token = t_ref[...]
    new = lax.dot_general(q, nk_ref[0], dims, preferred_element_type=jnp.float32) * scale
    new = jnp.where(token <= c_ref[...], new + slope * token.astype(jnp.float32), floor_score)
    top = jnp.maximum(jnp.max(old, axis=1, keepdims=True), jnp.max(new, axis=1, keepdims=True))
    top = jnp.maximum(top, 0.1 * floor_score)
    old = jnp.exp(old - top)
    new = jnp.exp(new - top)
    total = jnp.sum(old, axis=1, keepdims=True) + jnp.sum(new, axis=1, keepdims=True)
    accum = jnp.dot(old.astype(jnp.bfloat16), ov_ref[0], preferred_element_type=jnp.float32)
    accum += jnp.dot(new.astype(jnp.bfloat16), nv_ref[0], preferred_element_type=jnp.float32)
    some = total > 0
    safe = jnp.where(some, total, 1.0)
    part_ref[0] = (accum / safe).astype(part_ref.dtype)
    level = jnp.where(some, top + jnp.log(safe), floor_score)
    lane = lax.broadcasted_iota(jnp.int32, level_ref.shape[1:], 1)

    @pl.when(h == 0)
    def _():
        level_ref[...] = jnp.zeros_like(level_ref)

    level_ref[0] = jnp.where(lane == h, level, level_ref[0])


def attend(info, slopes, q, old_k, old_v, new_k, new_v, tokens, own_tokens, heads):
    requests, rows, width = q.shape
    size = width // heads
    head = lambda n: pl.BlockSpec((1, n, size), lambda r, h, *_: (r, 0, h))
    fixed = lambda shape: pl.BlockSpec(shape, lambda r, h, *_: (0, 0))
    block, own = old_k.shape[1], new_k.shape[1]
    lanes = 128
    part, level = pl.pallas_call(
        functools.partial(attend_kernel, 1.0 / math.sqrt(size)),
        grid_spec=pltpu.PrefetchScalarGridSpec(
            num_scalar_prefetch=2,
            grid=(requests, heads),
            in_specs=[
                head(rows),
                head(block),
                head(block),
                head(own),
                head(own),
                fixed((rows, 1)),
                fixed((1, own)),
            ],
            out_specs=[head(rows), pl.BlockSpec((1, rows, lanes), lambda r, h, *_: (r, 0, 0))],
        ),
        out_shape=[
            jax.ShapeDtypeStruct((requests, rows, width), jnp.bfloat16),
            jax.ShapeDtypeStruct((requests, rows, lanes), jnp.float32),
        ],
        compiler_params=pltpu.CompilerParams(vmem_limit_bytes=32 * 1024 * 1024),
        cost_estimate=pl.CostEstimate(
            flops=4 * requests * rows * (block + own) * width,
            bytes_accessed=4 * requests * (block + own + rows) * width,
            transcendentals=requests * rows * (block + own) * heads,
        ),
    )(info, slopes, q, old_k, old_v, new_k, new_v, tokens[:, None], own_tokens[None, :])
    return part, level[:, :, :heads]


def shards(hidden, ln_gain, w_qkv, w_out, kv_cache, cache_len):
    local_rows = hidden.shape[0]
    gx_n = lax.axis_size("gx")
    gy_n = lax.axis_size("gy")
    gy = lax.axis_index("gy")
    hidden_f = hidden.astype(jnp.float32)
    piece = local_rows // CHUNKS
    gathered = [
        lax.all_gather(hidden[c * piece : (c + 1) * piece], "gx", axis=0) for c in range(CHUNKS)
    ]
    sums = sum_gy(jnp.stack([jnp.sum(hidden_f, axis=1), jnp.sum(hidden_f * hidden_f, axis=1)]))
    mean = sums[0] / D
    rstd = lax.rsqrt(sums[1] / D - mean * mean + norm_eps)
    stats = lax.all_gather(jnp.stack([mean, rstd]), "gx", axis=0)
    stats, split_from = lax.optimization_barrier((stats, kv_cache))
    old_keys, old_values = split_cache(split_from)

    depth, local_heads = w_qkv.shape[:2]
    head_size = w_qkv.shape[2] // 3
    width = local_heads * head_size
    w_q = w_qkv[:, :, :head_size].reshape(depth, width)
    w_k = w_qkv[:, :, head_size : 2 * head_size].reshape(depth, width)
    w_v = w_qkv[:, :, 2 * head_size :].reshape(depth, width)

    requests = cache_len.shape[0]
    share = gx_n // requests
    group = share * local_rows
    rows = share * piece
    own_rows = rows // gy_n
    block = kv_cache.shape[1]
    queries, keys, values = [], [], []
    for c in range(CHUNKS):
        st = stats[:, :, c * piece : (c + 1) * piece]
        normed = (
            (gathered[c].astype(jnp.float32) - st[:, 0, :, None]) * st[:, 1, :, None] * ln_gain
        ).astype(jnp.bfloat16)
        normed = normed.reshape(gx_n * piece, depth)
        kv = [
            jnp.dot(normed, w, preferred_element_type=jnp.float32)
            .astype(jnp.bfloat16)
            .reshape(requests, rows, width)
            for w in (w_k, w_v)
        ]
        q = jnp.dot(normed, w_q, preferred_element_type=jnp.float32).astype(jnp.bfloat16)
        keys.append(scatter_gy(kv[0]))
        values.append(scatter_gy(kv[1]))
        queries.append(sum_gy(q).reshape(requests, rows, width))
        if c + 1 < CHUNKS:
            keys, values, queries, old_keys, old_values, gathered[c + 1] = (
                lax.optimization_barrier(
                    (keys, values, queries, old_keys, old_values, gathered[c + 1])
                )
            )

    flat = jnp.arange(rows, dtype=jnp.int32)
    tokens = [(flat // piece) * local_rows + c * piece + flat % piece for c in range(CHUNKS)]
    own = [lax.dynamic_slice_in_dim(t, gy * own_rows, own_rows) for t in tokens]
    own_tokens = jnp.concatenate(own)
    own_keys = jnp.concatenate(keys, axis=1)
    own_values = jnp.concatenate(values, axis=1)

    def whole(parts):
        full = lax.all_gather(parts, "gy", axis=0)
        full = full.reshape(gy_n, requests, CHUNKS, own_rows, width).transpose(1, 2, 0, 3, 4)
        full = full.reshape(requests, CHUNKS, share, piece, width).transpose(0, 2, 1, 3, 4)
        return full.reshape(requests, group, width)

    sent_keys, sent_values, queries = lax.optimization_barrier((own_keys, own_values, queries))
    fresh = jnp.stack([whole(sent_keys), whole(sent_values)], axis=2)
    window = min(group, block)
    padded = jnp.pad(fresh, ((0, 0), (window, window), (0, 0), (0, 0)))
    updated = kv_cache
    for r in range(requests):
        away = cache_len[r] - gy * block
        begin = jnp.clip(away, 0, block - window)
        taken = lax.dynamic_slice_in_dim(
            padded[r], jnp.clip(window + begin - away, 0, group + window), window
        )
        offset = begin - away + jnp.arange(window, dtype=jnp.int32)
        inside = (offset >= 0) & (offset < group)
        old = lax.dynamic_slice_in_dim(kv_cache[r], begin, window)
        new = jnp.where(inside[:, None, None], taken, old)
        updated = lax.dynamic_update_slice(updated, new[None], (r, begin, 0, 0))

    head_ids = lax.axis_index("gx") * local_heads + jnp.arange(local_heads, dtype=jnp.int32)
    slopes = jnp.exp2(-8.0 * (head_ids + 1).astype(jnp.float32) / (local_heads * gx_n))
    info = jnp.concatenate([(gy * block)[None].astype(jnp.int32), cache_len])
    results = []
    for c in range(CHUNKS):
        part, level = attend(
            info,
            slopes,
            queries[c],
            old_keys,
            old_values,
            own_keys,
            own_values,
            tokens[c],
            own_tokens,
            local_heads,
        )
        attn = combine(part, level).reshape(requests * rows, width)
        projected = lax.psum_scatter(
            jnp.dot(attn, w_out, preferred_element_type=jnp.float32).astype(jnp.bfloat16),
            "gx",
            scatter_dimension=0,
            tiled=True,
        ).astype(jnp.float32)
        results.append(projected)
    mixed = (jnp.concatenate(results) + hidden_f).astype(jnp.bfloat16)
    return (mixed, updated)


def solution(mesh):
    in_specs = (
        P(("req", "gx"), "gy"),
        P("gy"),
        P("gy", "gx", None),
        P("gx", "gy"),
        P("req", "gy", None, "gx"),
        P("req"),
    )
    out_specs = (P(("req", "gx"), "gy"), P("req", "gy", None, "gx"))
    return jax.shard_map(shards, mesh=mesh, in_specs=in_specs, out_specs=out_specs, check_vma=False)
```
